32 devices in a mesh: section: 2 (over core), shard: 4 (over z), replica: 4 (over y, x).
Axes of the slice: x: 2, y: 2, z: 4, core: 2. Of those that a mesh axis runs over, the one named last changes fastest.
Arguments:
- edges: bfloat16 [2, 2, 4, 1024, 896], P('section', None, 'replica', 'shard'), may hold values from -6 to 6
- positions: int32 [2, 4, 1024], P(None, 'replica', 'shard'), may hold values from 0 to 767, as said below
- attn_in: bfloat16 [2, 896, 1152], P('section', 'shard'), may hold values from -0.1875 to 0.1875
- out_proj: bfloat16 [2, 896, 896], P('section', 'shard'), may hold values from -1.5 to 1.5
- mlp_in: bfloat16 [2, 896, 9728], P('section', 'shard'), may hold values from -0.1875 to 0.1875
- mlp_out: bfloat16 [2, 4864, 896], P('section', 'shard'), may hold values from -0.078125 to 0.078125
- gains: bfloat16 [2, 1792], P('section', 'shard'), may hold values from 0.5 to 1.5
- bias: bfloat16 [2, 1152], P('section', 'shard'), may hold values from -3 to 3
Outputs:
- layer_outputs: bfloat16 [2, 2, 4, 1024, 896], P('section', None, 'replica', 'shard')
- input_grads: float32 [2, 2, 4, 1024, 896], P('section', None, 'replica', 'shard')
- grad_attn_in: float32 [2, 896, 1152], P('section', 'shard')
- grad_out_proj: float32 [2, 896, 896], P('section', 'shard')
- grad_mlp_in: float32 [2, 896, 9728], P('section', 'shard')
- grad_mlp_out: float32 [2, 4864, 896], P('section', 'shard')
- grad_gains: float32 [2, 1792], P('section', 'shard')
- grad_bias: float32 [2, 1024], P('section', 'shard')
- grad_value_bias: float32 [2, 128], P('section', 'shard')
The draws below stay inside these ranges and needn't reach their ends.
Inputs may be any that keep to these rules, and one draw needn't show every extreme that they name: In each sequence of 1024 tokens the positions run 0, 1, 2, ... and restart at 0 exactly once, at a token between 256 and 768; in some sequence the restart is at token 768.
All inputs are finite; a program needn't handle non-finite values.
Results may differ from the reference program's by a relative error of at most 0.023.
Values may be sent and summed in bfloat16 or wider, within the bound.
A program may use at most 384 MiB of HBM per device.

```python
import math
import jax
import jax.numpy as jnp
from jax import lax

D = 896
QUERY_HEADS = 14
KEY_VALUE_HEADS = 2
HEAD_SIZE = 64
FF = 4864
QKV = 1152
SEQ = 1024
MICRO = 2
SEQS = 4
LAYERS = 2


def draw_positions(key, part):
    first_key = jax.random.fold_in(key, 11)
    second_key = jax.random.fold_in(key, 23)
    restarts = jax.random.randint(first_key, (MICRO * SEQS,), SEQ // 4, 3 * SEQ // 4 + 1).astype(jnp.int32)
    pick = jax.random.randint(second_key, (), 0, MICRO * SEQS).astype(jnp.int32)
    slots = jnp.arange(MICRO * SEQS, dtype=jnp.int32)
    restarts = jnp.where(slots == pick, 3 * SEQ // 4, restarts).astype(jnp.int32)
    restarts = restarts.reshape(MICRO, SEQS, 1)
    indices = jnp.arange(SEQ, dtype=jnp.int32)[None, None, :]
    return jnp.where(indices < restarts, indices, indices - restarts).astype(jnp.int32)


def block_levels(rng, dims, pieces, low, top_value):
    gain, own = 1.0, jax.random.fold_in(rng, 6)
    for axis_at, shards_of in pieces:
        heights = jnp.exp(jax.random.uniform(jax.random.fold_in(own, axis_at), (shards_of,), jnp.float32, low / len(pieces), top_value / len(pieces)))
        gain = gain * jnp.repeat(heights, dims[axis_at] // shards_of).reshape([-1 if axis == axis_at else 1 for axis in range(len(dims))])
    return gain


def scatter_about(key, shape, spread, reach, pieces=(), kind=jnp.bfloat16):
    result = jax.random.normal(key, shape, jnp.float32) * spread
    if len(pieces) > 0:
        result = block_levels(key, shape, pieces, -0.22, 0.18) * result
    return jnp.clip(result, min=-reach, max=reach).astype(kind)


def setup_inputs(seed: int = 0) -> dict:
    key_of = jax.random.split(jax.random.key(seed), 9)
    return {
        "edges": scatter_about(key_of[0], (2, MICRO, SEQS, SEQ, D), 1.0, 6.0, ((0, 2), (2, 4), (3, 4))),
        "positions": draw_positions(jax.random.fold_in(key_of[8], 71), 0),
        "attn_in": scatter_about(key_of[2], (LAYERS, D, QKV), D ** -0.5, 0.1875, ((0, 2), (1, 4))),
        "out_proj": scatter_about(key_of[3], (LAYERS, D, D), (max(1, D * 16 // SEQ)) ** -0.5, 1.5, ((0, 2), (1, 4))),
        "mlp_in": scatter_about(key_of[4], (LAYERS, D, 2 * FF), D ** -0.5, 0.1875, ((0, 2), (1, 4))),
        "mlp_out": scatter_about(key_of[5], (LAYERS, FF, D), FF ** -0.5, 0.078125, ((0, 2), (1, 4))),
        "gains": jnp.clip(1.0 + 0.1 * jax.random.normal(key_of[6], (LAYERS, 2 * D), jnp.float32), 0.5, 1.5).astype(jnp.bfloat16),
        "bias": scatter_about(key_of[7], (LAYERS, QKV), 0.5, 3.0, ((0, 2), (1, 4))),
    }


@jax.custom_vjp
def lower_precision(v):
    return lax.optimization_barrier(v.astype(jnp.bfloat16)).astype(jnp.float32)

@jax.custom_vjp
def low_back(v):
    return v

def low_keep(v):
    return (lower_precision(v), None)

def low_pass(kept, grad):
    return (grad,)

def back_keep(v):
    return (v, None)

def back_low(kept, grad):
    return (lower_precision(grad),)
lower_precision.defvjp(low_keep, low_pass)
low_back.defvjp(back_keep, back_low)
eps_norm = 1e-06
rope_base = 1000000.0
precise = lax.Precision.HIGHEST

def matmul(first_mat, second_mat):
    return jnp.dot(first_mat, second_mat, precision=precise, preferred_element_type=jnp.float32)

def rotary_tables(token_pos):
    half_dim = HEAD_SIZE // 2
    frequency = jnp.power(rope_base, -2.0 * jnp.arange(half_dim, dtype=jnp.float32) / HEAD_SIZE)
    angles = token_pos.astype(jnp.float32)[:, None] * frequency[None, :]
    return (jnp.cos(angles)[:, None, :], jnp.sin(angles)[:, None, :])

def rotary_embed(values, cosine_table, sine_values):
    half_dim = values.shape[-1] // 2
    first_half = values[..., :half_dim]
    second_half = values[..., half_dim:]
    return jnp.concatenate([first_half * cosine_table - second_half * sine_values, second_half * cosine_table + first_half * sine_values], axis=-1)

def rms_scale(values, gain_part):
    return values * lax.rsqrt(lax.optimization_barrier(jnp.mean(values * values, axis=-1, keepdims=True)) + eps_norm) * gain_part

def block_layer(hidden, weights, token_pos):
    attn_full, out_full, mlp_full, down_full, gain_full, bias_full = weights
    length_total = hidden.shape[0]
    heads_per_group = QUERY_HEADS // KEY_VALUE_HEADS
    scaling = 1.0 / math.sqrt(HEAD_SIZE)
    normed = lower_precision(rms_scale(hidden, gain_full[:D]))
    project_matrix = low_back(matmul(normed, attn_full) + bias_full)
    cosine_table, sine_values = rotary_tables(token_pos)
    query_rows = lower_precision(rotary_embed(project_matrix[:, :QUERY_HEADS * HEAD_SIZE].reshape(length_total, QUERY_HEADS, HEAD_SIZE), cosine_table, sine_values))
    keys_rotated = lower_precision(rotary_embed(project_matrix[:, QUERY_HEADS * HEAD_SIZE:(QUERY_HEADS + KEY_VALUE_HEADS) * HEAD_SIZE].reshape(length_total, KEY_VALUE_HEADS, HEAD_SIZE), cosine_table, sine_values))
    value_rows_every = lower_precision(project_matrix[:, (QUERY_HEADS + KEY_VALUE_HEADS) * HEAD_SIZE:].reshape(length_total, KEY_VALUE_HEADS, HEAD_SIZE))
    grouped_heads = query_rows.reshape(length_total, KEY_VALUE_HEADS, heads_per_group, HEAD_SIZE)
    scores = low_back(jnp.einsum('igkd,jgd->gkij', grouped_heads, keys_rotated, precision=precise) * scaling)
    indices = jnp.arange(length_total, dtype=jnp.int32)
    allowed = (indices[None, :] <= indices[:, None]) & (indices[None, :] >= (indices - token_pos)[:, None])
    masked = jnp.where(allowed[None, None], scores, -1e+30)
    row_max = lax.optimization_barrier(jnp.max(masked, axis=-1, keepdims=True))
    exponent = jnp.exp(masked - row_max)
    probability = lower_precision(exponent / lax.optimization_barrier(jnp.sum(exponent, axis=-1, keepdims=True)))
    attended = jnp.einsum('gkij,jgd->igkd', probability, value_rows_every, precision=precise).reshape(length_total, QUERY_HEADS * HEAD_SIZE)
    attended = lower_precision(low_back(attended))
    middle = hidden + low_back(matmul(attended, out_full))
    normed_two = lower_precision(rms_scale(middle, gain_full[D:]))
    gate_up = low_back(matmul(normed_two, mlp_full))
    activated = lower_precision(jax.nn.silu(gate_up[:, :FF]) * gate_up[:, FF:])
    return middle + low_back(matmul(activated, down_full))

def reference(edges, positions, attn_in, out_proj, mlp_in, mlp_out, gains, bias):
    weight_sets = []
    for layer_id in range(LAYERS):
        weight_sets.append(tuple((stacked[layer_id].astype(jnp.float32) for stacked in (attn_in, out_proj, mlp_in, mlp_out, gains, bias))))
    seq_count = MICRO * SEQS
    inputs_all = edges[0].reshape(seq_count, SEQ, D)
    cotangents = edges[1].reshape(seq_count, SEQ, D)
    all_pos = positions.reshape(seq_count, SEQ).astype(jnp.int32)
    zero_grads = jax.tree.map(jnp.zeros_like, (weight_sets[0], weight_sets[1]))

    def one_sequence(running, inputs_now):
        block_in, cotangent, token_pos = inputs_now

        def apply_layer(hidden, weights):
            return block_layer(hidden, weights, token_pos)
        first_out, first_back = jax.vjp(apply_layer, block_in.astype(jnp.float32), weight_sets[0])
        sent = lower_precision(first_out)
        second_out, second_back = jax.vjp(apply_layer, sent, weight_sets[1])
        middle_grad, second_grads = second_back(cotangent.astype(jnp.float32))
        input_grad, first_grads = first_back(lower_precision(middle_grad))
        running = jax.tree.map(lambda kept_sum, addend: kept_sum + addend, running, (first_grads, second_grads))
        return (running, (sent.astype(jnp.bfloat16), second_out.astype(jnp.bfloat16), input_grad, middle_grad))
    running, results = lax.scan(one_sequence, zero_grads, (inputs_all, cotangents, all_pos))
    sent_all, block_out, input_grad, middle_grad = results
    layer_outputs = jnp.stack([sent_all, block_out]).reshape(2, MICRO, SEQS, SEQ, D)
    input_grads = jnp.stack([input_grad, middle_grad]).reshape(2, MICRO, SEQS, SEQ, D)
    stacked_grads = [jnp.stack([running[0][field_id], running[1][field_id]]) for field_id in range(6)]
    query_key = (QUERY_HEADS + KEY_VALUE_HEADS) * HEAD_SIZE
    return (layer_outputs, input_grads, stacked_grads[0], stacked_grads[1], stacked_grads[2], stacked_grads[3], stacked_grads[4], stacked_grads[5][:, :query_key], stacked_grads[5][:, query_key:])
```

```python
import math

import jax
import jax.numpy as jnp
from jax import lax
from jax.experimental import pallas as pl
from jax.experimental.pallas import tpu as pltpu
from jax.sharding import PartitionSpec as P

D = 896
QUERY_HEADS = 14
KEY_VALUE_HEADS = 2
HEAD_SIZE = 64
FF = 4864
QKV = 1152


eps_norm = 1e-06
rope_base = 1000000.0


def brain_float(values):
    return values.astype(jnp.bfloat16)


def matmul(first_mat, second_mat):
    return jnp.dot(first_mat, second_mat, preferred_element_type=jnp.float32)


def matmul_left(first_mat, second_mat):
    return lax.dot_general(
        first_mat, second_mat, (((0,), (0,)), ((), ())), preferred_element_type=jnp.float32
    )


def matmul_right(first_mat, second_mat):
    return lax.dot_general(
        first_mat, second_mat, (((1,), (1,)), ((), ())), preferred_element_type=jnp.float32
    )


def rotary_tables(token_pos):
    half_dim = HEAD_SIZE // 2
    frequency = jnp.power(rope_base, -2.0 * jnp.arange(half_dim, dtype=jnp.float32) / HEAD_SIZE)
    angles = token_pos.astype(jnp.float32)[:, None] * frequency[None, :]
    return (jnp.cos(angles)[:, None, :], jnp.sin(angles)[:, None, :])


def rotary_embed(values, cosine_table, sine_values):
    half_dim = values.shape[-1] // 2
    first_half = values[..., :half_dim]
    second_half = values[..., half_dim:]
    return jnp.concatenate(
        [
            first_half * cosine_table - second_half * sine_values,
            second_half * cosine_table + first_half * sine_values,
        ],
        axis=-1,
    )


def rotary_backward(grads, cosine_table, sine_values):
    half_dim = grads.shape[-1] // 2
    first_half = grads[..., :half_dim]
    second_half = grads[..., half_dim:]
    return jnp.concatenate(
        [
            first_half * cosine_table + second_half * sine_values,
            second_half * cosine_table - first_half * sine_values,
        ],
        axis=-1,
    )


def visible(token_pos, row_index, seq_len):
    columns = jnp.arange(seq_len, dtype=jnp.int32)
    return (columns[None, :] <= row_index[:, None]) & (
        columns[None, :] >= (row_index - token_pos)[:, None]
    )


def attention_inputs(block_in, token_pos, weights):
    attn_full, out_full, mlp_full, down_full, gain_full, bias_full = weights
    count_of_rows = block_in.shape[0]
    hidden = block_in.astype(jnp.float32)
    inverse = lax.rsqrt(jnp.mean(hidden * hidden, axis=-1, keepdims=True) + eps_norm)
    normed = brain_float(hidden * inverse * gain_full[:D].astype(jnp.float32))
    project_matrix = matmul(normed, attn_full) + bias_full.astype(jnp.float32)
    cosine_table, sine_values = rotary_tables(token_pos)
    query_rows = brain_float(
        rotary_embed(
            project_matrix[:, : QUERY_HEADS * HEAD_SIZE].reshape(
                count_of_rows, QUERY_HEADS, HEAD_SIZE
            ),
            cosine_table,
            sine_values,
        )
    ).reshape(count_of_rows, QUERY_HEADS * HEAD_SIZE)
    keys_here = brain_float(
        rotary_embed(
            project_matrix[
                :, QUERY_HEADS * HEAD_SIZE : (QUERY_HEADS + KEY_VALUE_HEADS) * HEAD_SIZE
            ].reshape(count_of_rows, KEY_VALUE_HEADS, HEAD_SIZE),
            cosine_table,
            sine_values,
        )
    ).reshape(count_of_rows, KEY_VALUE_HEADS * HEAD_SIZE)
    value_rows_local = brain_float(project_matrix[:, (QUERY_HEADS + KEY_VALUE_HEADS) * HEAD_SIZE :])
    return (normed, inverse, query_rows, keys_here, value_rows_local)


def attention_forward(query_rows, keys_all, value_rows_every, allowed):
    count_of_rows = query_rows.shape[0]
    heads_per_group = QUERY_HEADS // KEY_VALUE_HEADS
    scaling = 1.0 / math.sqrt(HEAD_SIZE)
    grouped_heads = query_rows.reshape(count_of_rows, KEY_VALUE_HEADS, heads_per_group, HEAD_SIZE)
    outputs = []
    logsums = []
    for head_cluster in range(KEY_VALUE_HEADS):
        keys_group = keys_all[:, head_cluster * HEAD_SIZE : (head_cluster + 1) * HEAD_SIZE]
        values_group = value_rows_every[
            :, head_cluster * HEAD_SIZE : (head_cluster + 1) * HEAD_SIZE
        ]
        scores = (
            jnp.einsum(
                "ikd,jd->kij",
                grouped_heads[:, head_cluster],
                keys_group,
                preferred_element_type=jnp.float32,
            )
            * scaling
        )
        masked = jnp.where(allowed[None], scores, -1e30)
        row_max = jnp.max(masked, axis=-1, keepdims=True)
        exponent = jnp.exp(masked - row_max)
        row_sum = jnp.sum(exponent, axis=-1, keepdims=True)
        probability = brain_float(exponent / row_sum)
        outputs.append(
            jnp.einsum("kij,jd->ikd", probability, values_group, preferred_element_type=jnp.float32)
        )
        logsums.append((row_max + jnp.log(row_sum))[..., 0])
    return (
        jnp.stack(outputs, axis=1).reshape(count_of_rows, QUERY_HEADS * HEAD_SIZE),
        jnp.stack(logsums, axis=0),
    )


def attention_backward(query_rows, keys_all, value_rows_every, logsum, attended_gradient, allowed):
    count_of_rows = query_rows.shape[0]
    heads_per_group = QUERY_HEADS // KEY_VALUE_HEADS
    scaling = 1.0 / math.sqrt(HEAD_SIZE)
    grouped_heads = query_rows.reshape(count_of_rows, KEY_VALUE_HEADS, heads_per_group, HEAD_SIZE)
    grouped_gradient = attended_gradient.reshape(
        count_of_rows, KEY_VALUE_HEADS, heads_per_group, HEAD_SIZE
    )
    query_parts = []
    key_parts = []
    value_parts = []
    for head_cluster in range(KEY_VALUE_HEADS):
        keys_group = keys_all[:, head_cluster * HEAD_SIZE : (head_cluster + 1) * HEAD_SIZE]
        values_group = value_rows_every[
            :, head_cluster * HEAD_SIZE : (head_cluster + 1) * HEAD_SIZE
        ]
        scores = (
            jnp.einsum(
                "ikd,jd->kij",
                grouped_heads[:, head_cluster],
                keys_group,
                preferred_element_type=jnp.float32,
            )
            * scaling
        )
        masked = jnp.where(allowed[None], scores, -1e30)
        probability = jnp.exp(masked - logsum[head_cluster][..., None])
        value_parts.append(
            jnp.einsum(
                "kij,ikd->jd",
                brain_float(probability),
                grouped_gradient[:, head_cluster],
                preferred_element_type=jnp.float32,
            )
        )
        prob_grad = jnp.einsum(
            "ikd,jd->kij",
            grouped_gradient[:, head_cluster],
            values_group,
            preferred_element_type=jnp.float32,
        )
        inner_sum = jnp.sum(probability * prob_grad, axis=-1, keepdims=True)
        score_low = brain_float(probability * (prob_grad - inner_sum))
        query_parts.append(
            jnp.einsum("kij,jd->ikd", score_low, keys_group, preferred_element_type=jnp.float32)
            * scaling
        )
        key_parts.append(
            jnp.einsum(
                "kij,ikd->jd",
                score_low,
                grouped_heads[:, head_cluster],
                preferred_element_type=jnp.float32,
            )
            * scaling
        )
    return (
        jnp.stack(query_parts, axis=1).reshape(count_of_rows, QUERY_HEADS * HEAD_SIZE),
        jnp.concatenate(key_parts, axis=1),
        jnp.concatenate(value_parts, axis=1),
    )


def finish_forward(block_in, token_pos, row_index, first_part, keys_all, value_rows_every, weights):
    attn_full, out_full, mlp_full, down_full, gain_full, bias_full = weights
    normed, inverse, query_rows, keys_here, value_rows_local = first_part
    allowed = visible(token_pos, row_index, keys_all.shape[0])
    attended, logsum = attention_forward(query_rows, keys_all, value_rows_every, allowed)
    attended_low = brain_float(attended)
    middle = block_in.astype(jnp.float32) + matmul(attended_low, out_full)
    inverse_two = lax.rsqrt(jnp.mean(middle * middle, axis=-1, keepdims=True) + eps_norm)
    normed_two = brain_float(middle * inverse_two * gain_full[D:].astype(jnp.float32))
    gate_up = matmul(normed_two, mlp_full)
    activated = brain_float(jax.nn.silu(gate_up[:, :FF]) * gate_up[:, FF:])
    result = brain_float(middle + matmul(activated, down_full))
    return (result, logsum, attended_low, middle, inverse_two, normed_two, gate_up, activated)


def backward_mlp(cotangent, saved_now, weights):
    attn_full, out_full, mlp_full, down_full, gain_full, bias_full = weights
    second_part = saved_now[5]
    result, logsum, attended_low, middle, inverse_two, normed_two, gate_up, activated = second_part
    mid_grad = matmul_right(cotangent, down_full)
    gate_in = gate_up[:, :FF]
    upward = gate_up[:, FF:]
    sigmoid_g = jax.nn.sigmoid(gate_in)
    gate_grad = mid_grad * upward * sigmoid_g * (1.0 + gate_in * (1.0 - sigmoid_g))
    up_grad = mid_grad * gate_in * sigmoid_g
    gate_up_low = brain_float(jnp.concatenate([gate_grad, up_grad], axis=1))
    normed_grad = matmul_right(gate_up_low, mlp_full)
    return (gate_up_low, normed_grad)


def backward_branches(cotangent, mlp_part, saved_now, row_index, weights):
    attn_full, out_full, mlp_full, down_full, gain_full, bias_full = weights
    block_in, token_pos, first_part, keys_all, value_rows_every, second_part = saved_now
    normed, inverse, query_rows, keys_here, value_rows_local = first_part
    result, logsum, attended_low, middle, inverse_two, normed_two, gate_up, activated = second_part
    gate_up_low, normed_grad = mlp_part
    plain_two = middle * inverse_two
    gain_grad_two = jnp.sum(normed_grad * plain_two, axis=0)
    scaled_two = normed_grad * gain_full[D:].astype(jnp.float32)
    middle_grad = cotangent.astype(jnp.float32) + inverse_two * (
        scaled_two - plain_two * jnp.mean(scaled_two * plain_two, axis=-1, keepdims=True)
    )
    branch_low = brain_float(middle_grad)
    attended_gradient = brain_float(matmul_right(branch_low, out_full))
    allowed = visible(token_pos, row_index, keys_all.shape[0])
    query_grad, key_part, value_part = attention_backward(
        query_rows, keys_all, value_rows_every, logsum, attended_gradient, allowed
    )
    return (query_grad, key_part, value_part, middle_grad, branch_low, gate_up_low, gain_grad_two)


def backward_inputs(back_part, key_gradients, value_grads, saved_now, weights):
    attn_full, out_full, mlp_full, down_full, gain_full, bias_full = weights
    block_in, token_pos, first_part, keys_all, value_rows_every, second_part = saved_now
    normed, inverse, query_rows, keys_here, value_rows_local = first_part
    query_grad, key_part, value_part, middle_grad, branch_low, gate_up_low, gain_grad_two = (
        back_part
    )
    count_of_rows = block_in.shape[0]
    cosine_table, sine_values = rotary_tables(token_pos)
    query_back = rotary_backward(
        query_grad.reshape(count_of_rows, QUERY_HEADS, HEAD_SIZE), cosine_table, sine_values
    ).reshape(count_of_rows, QUERY_HEADS * HEAD_SIZE)
    key_backward = rotary_backward(
        key_gradients.reshape(count_of_rows, KEY_VALUE_HEADS, HEAD_SIZE), cosine_table, sine_values
    ).reshape(count_of_rows, KEY_VALUE_HEADS * HEAD_SIZE)
    project_low = brain_float(jnp.concatenate([query_back, key_backward, value_grads], axis=1))
    bias_grad = jnp.sum(project_low, axis=0, dtype=jnp.float32)
    normed_grad = matmul_right(project_low, attn_full)
    plain_one = block_in.astype(jnp.float32) * inverse
    gain_grad_one = jnp.sum(normed_grad * plain_one, axis=0)
    scaled_one = normed_grad * gain_full[:D].astype(jnp.float32)
    input_grad = middle_grad + inverse * (
        scaled_one - plain_one * jnp.mean(scaled_one * plain_one, axis=-1, keepdims=True)
    )
    return (input_grad, project_low, jnp.concatenate([gain_grad_one, gain_grad_two]), bias_grad)


MESH = pl.DeviceIdType.MESH


def gather_kernel(
    a_in, m_in, o_in, a_out, m_out, o_out, here, zs, zr, rs, rr, ds, dr, own_s, own_r, cs, cr
):
    section = lax.axis_index("section")
    shard = lax.axis_index("shard")
    replica = lax.axis_index("replica")
    nz = lax.axis_size("shard")
    other = 1 - section
    near = replica + 1 - 2 * lax.rem(replica, 2)
    far = lax.rem(replica + 2, 4)
    across = 3 - replica
    a_cols = a_in.shape[1] // 4
    m_cols = m_in.shape[2] // 4

    def piece(p, layer, z, q):
        if p == 0:
            return a_out.at[layer, z, :, pl.ds(pl.multiple_of(q * a_cols, 128), a_cols)]
        if p == 3:
            return o_out.at[layer, z, q]
        return m_out.at[layer, z, p - 1, :, pl.ds(pl.multiple_of(q * m_cols, 128), m_cols)]

    def source(p, q):
        if p == 0:
            return a_in.at[:, pl.ds(pl.multiple_of(q * a_cols, 128), a_cols)]
        if p == 3:
            return o_in.at[q]
        return m_in.at[p - 1, :, pl.ds(pl.multiple_of(q * m_cols, 128), m_cols)]

    def remote(src, dst, send, recv, target):
        return pltpu.make_async_remote_copy(
            src_ref=src,
            dst_ref=dst,
            send_sem=send,
            recv_sem=recv,
            device_id=target,
            device_id_type=MESH,
        )

    barrier = pltpu.get_barrier_semaphore()
    peers = [{"shard": lax.rem(shard + k, nz)} for k in range(1, nz)]
    peers += [{"replica": near}, {"replica": far}, {"section": other}]
    for peer in peers:
        pl.semaphore_signal(barrier, inc=1, device_id=peer, device_id_type=MESH)
    pl.semaphore_wait(barrier, len(peers))

    order = sorted(range(1, nz), key=lambda k: min(k, nz - k))
    sent = []

    def along(p, k):
        return remote(
            source(p, replica),
            piece(p, section, shard, replica),
            zs.at[p, k],
            zr.at[p, k],
            {"shard": lax.rem(shard + k, nz)},
        )

    for p in range(4):
        for k in order:
            copy = along(p, k)
            copy.start()
            sent.append(copy)
    wholes = (
        (a_in, a_out.at[section, shard], a_out.at[other, shard]),
        (m_in, m_out.at[section, shard], m_out.at[other, shard]),
        (o_in, o_out.at[section, shard], o_out.at[other, shard]),
    )
    locals_here = []
    arrivals = []
    for index, (src, dst, landing) in enumerate(wholes):
        copy = pltpu.make_async_copy(src, dst, here.at[index])
        copy.start()
        locals_here.append(copy)
        copy = remote(src, dst, own_s.at[index], own_r.at[index], {"section": other})
        copy.start()
        sent.append(copy)
        arrivals.append(
            remote(src, landing, own_s.at[index], own_r.at[index], {"section": other})
        )

    def to_core(p, k, kind, q):
        z = lax.rem(shard + nz - k, nz)
        ref = piece(p, section, z, q)
        copy = remote(ref, ref, cs.at[kind, p, k], cr.at[kind, p, k], {"section": other})
        copy.start()
        sent.append(copy)
        landing = piece(p, other, z, q)
        arrivals.append(
            remote(
                landing, landing, cs.at[kind, p, k], cr.at[kind, p, k], {"section": other}
            )
        )

    def first_hop(p, k):
        z = lax.rem(shard + nz - k, nz)
        ref = piece(p, section, z, replica)
        remote(ref, ref, zs.at[p, k], zr.at[p, k], {"shard": z}).wait_recv()
        for way, target in enumerate((near, far)):
            copy = remote(ref, ref, rs.at[way, p, k], rr.at[way, p, k], {"replica": target})
            copy.start()
            sent.append(copy)
        to_core(p, k, 0, replica)

    def second_hop(p, k):
        z = lax.rem(shard + nz - k, nz)
        by_near = (p + (k if p in (0, 3) else 0)) % 2 == 0
        for way, (origin, target) in enumerate(((near, far), (far, near))):
            ref = piece(p, section, z, origin)
            remote(
                ref, ref, rs.at[way, p, k], rr.at[way, p, k], {"replica": origin}
            ).wait_recv()
            if by_near == (way == 0):
                copy = remote(ref, ref, ds.at[p, k], dr.at[p, k], {"replica": target})
                copy.start()
                sent.append(copy)
            to_core(p, k, 1 + way, origin)

    def third_hop(p, k):
        z = lax.rem(shard + nz - k, nz)
        ref = piece(p, section, z, across)
        by_near = (p + (k if p in (0, 3) else 0)) % 2 == 0
        origin = far if by_near else near
        remote(ref, ref, ds.at[p, k], dr.at[p, k], {"replica": origin}).wait_recv()
        to_core(p, k, 3, across)

    for step in range(6):
        if step < 4:
            for k in order:
                first_hop(step, k)
        if 1 <= step < 5:
            for k in order:
                second_hop(step - 1, k)
        if step >= 2:
            for k in order:
                third_hop(step - 2, k)
    for copy in arrivals:
        copy.wait_recv()
    for copy in sent:
        copy.wait_send()
    for copy in locals_here:
        copy.wait()


def gather_weights(attn_in, out_proj, mlp_in, mlp_out):
    nz = lax.axis_size("shard")
    joined = jnp.concatenate([attn_in, out_proj], axis=1)
    rows, a_cols = joined.shape
    m_cols = mlp_in.shape[1]
    down_rows, d_model = mlp_out.shape
    m_in = mlp_in.reshape(2, rows // 2, m_cols)
    o_in = mlp_out.reshape(4, down_rows // 4, d_model)
    dma = pltpu.SemaphoreType.DMA
    a_all, m_all, o_all = pl.pallas_call(
        gather_kernel,
        out_shape=(
            jax.ShapeDtypeStruct((2, nz) + joined.shape, jnp.bfloat16),
            jax.ShapeDtypeStruct((2, nz) + m_in.shape, jnp.bfloat16),
            jax.ShapeDtypeStruct((2, nz) + o_in.shape, jnp.bfloat16),
        ),
        in_specs=[pl.BlockSpec(memory_space=pl.ANY)] * 3,
        out_specs=(pl.BlockSpec(memory_space=pl.ANY),) * 3,
        scratch_shapes=[
            dma((3,)),
            dma((4, nz)),
            dma((4, nz)),
            dma((2, 4, nz)),
            dma((2, 4, nz)),
            dma((4, nz)),
            dma((4, nz)),
            dma((3,)),
            dma((3,)),
            dma((4, 4, nz)),
            dma((4, 4, nz)),
        ],
        compiler_params=pltpu.CompilerParams(collective_id=0, has_side_effects=True),
    )(joined, m_in, o_in)
    return (
        a_all.reshape(2, nz * rows, a_cols),
        m_all.reshape(2, nz * rows, m_cols),
        o_all.reshape(2, nz * down_rows, d_model),
    )


def swap_cores(value):
    return lax.ppermute(value, "section", [(0, 1), (1, 0)])


def scatter_shards(value):
    nz = lax.axis_size("shard")
    shard = lax.axis_index("shard")
    total = lax.dynamic_index_in_dim(value, shard, 0, keepdims=False).astype(jnp.float32)
    for k in range(1, nz):
        block = lax.dynamic_index_in_dim(value, lax.rem(shard + k, nz), 0, keepdims=False)
        block = lax.ppermute(block, "shard", [(i, (i + k) % nz) for i in range(nz)])
        total = total + block.astype(jnp.float32)
    return brain_float(total)


def reduce_group(send, keep):
    half = brain_float(keep.astype(jnp.float32) + swap_cores(send).astype(jnp.float32))
    part = lax.psum_scatter(half, "replica", scatter_dimension=0, tiled=True)
    nz = lax.axis_size("shard")
    block = scatter_shards(part.reshape(nz, part.shape[0] // nz, part.shape[1]))
    return lax.all_gather(block, "replica", axis=0, tiled=True)


def replica_major(values, inner):
    nz = lax.axis_size("shard")
    rows = values.shape[0]
    width = values.shape[1] // (inner * 4 * nz)
    return (
        values.reshape(rows, nz, inner, 4, width)
        .transpose(0, 2, 3, 1, 4)
        .reshape(rows, values.shape[1])
    )


def picked(section_id, first, second):
    return jnp.where(section_id == 0, second, first), jnp.where(section_id == 0, first, second)


def mlp_weight_grads(section_id, normed_two, gate_up_low, activated, cotangent):
    nz = lax.axis_size("shard")
    normed_two = replica_major(normed_two, 1)
    send, keep = picked(section_id, gate_up_low[:, :FF], gate_up_low[:, FF:])
    grad_m = reduce_group(
        brain_float(matmul_left(normed_two, send)), brain_float(matmul_left(normed_two, keep))
    )
    send, keep = picked(section_id, cotangent[:, : D // 2], cotangent[:, D // 2 :])

    def down(half):
        grad = brain_float(matmul_left(activated, half))
        rows = grad.shape[0]
        return (
            grad.reshape(nz, 4, rows // (4 * nz), D // 2).transpose(1, 0, 2, 3).reshape(rows, D // 2)
        )

    return grad_m, reduce_group(down(send), down(keep))


def attention_weight_grads(section_id, normed, project_low, attended_low, branch_low):
    normed = replica_major(normed, 2)
    attended_low = replica_major(attended_low, 2)
    normed_send, normed_keep = picked(section_id, normed[:, : D // 2], normed[:, D // 2 :])
    attended_send, attended_keep = picked(
        section_id, attended_low[:, : D // 2], attended_low[:, D // 2 :]
    )

    def grads(first, second):
        return brain_float(
            jnp.concatenate(
                [matmul_left(first, project_low), matmul_left(second, branch_low)], axis=1
            )
        )

    return reduce_group(grads(normed_send, attended_send), grads(normed_keep, attended_keep))


def local(edges, positions, attn_in, out_proj, mlp_in, mlp_out, gains, bias):
    section_id = lax.axis_index("section")
    shard_id = lax.axis_index("shard")
    count_of_rows = edges.shape[3]
    first = section_id == 0
    own = edges[0, :, 0]
    incoming = swap_cores(jnp.where(first, own[1], own[0]))
    block_in = jnp.where(first, own[0], incoming)
    cotangent = jnp.where(first, incoming, own[1])
    token_pos = lax.dynamic_index_in_dim(positions[:, 0], section_id, 0, keepdims=False)
    row_index = shard_id * count_of_rows + jnp.arange(count_of_rows, dtype=jnp.int32)
    gain_rows = gains.shape[1]
    vectors = lax.all_gather(
        jnp.concatenate([gains[0], bias[0]]), ("section", "shard"), axis=0, tiled=False
    ).reshape(2, -1, gain_rows + bias.shape[1])
    gain_full = vectors[:, :, :gain_rows].reshape(2, -1)
    bias_full = vectors[:, :, gain_rows:].reshape(2, -1)
    a_all, m_all, o_all = gather_weights(attn_in[0], out_proj[0], mlp_in[0], mlp_out[0])
    weights = [
        (a_all[l][:, :QKV], a_all[l][:, QKV:], m_all[l], o_all[l], gain_full[l], bias_full[l])
        for l in range(2)
    ]
    saved_all = []
    outputs = []
    key_width = KEY_VALUE_HEADS * HEAD_SIZE
    for layer in range(2):
        first_part = attention_inputs(block_in, token_pos, weights[layer])
        both = lax.all_gather(
            jnp.concatenate([first_part[3], first_part[4]], axis=1), "shard", axis=0, tiled=True
        )
        keys_all, values_all = both[:, :key_width], both[:, key_width:]
        second_part = finish_forward(
            block_in, token_pos, row_index, first_part, keys_all, values_all, weights[layer]
        )
        saved_all.append((block_in, token_pos, first_part, keys_all, values_all, second_part))
        block_in = second_part[0]
        outputs.append(block_in)
    grads_out = [None, None]
    reduced = [None, None]
    small = [None, None]
    for layer in (1, 0):
        saved_now = saved_all[layer]
        first_saved, second_saved = saved_now[2], saved_now[5]
        mlp_part = backward_mlp(cotangent, saved_now, weights[layer])
        grad_m, grad_o = mlp_weight_grads(
            section_id, second_saved[5], mlp_part[0], second_saved[7], cotangent
        )
        back_part = backward_branches(cotangent, mlp_part, saved_now, row_index, weights[layer])
        both = lax.psum_scatter(
            brain_float(jnp.concatenate([back_part[1], back_part[2]], axis=1)),
            "shard",
            scatter_dimension=0,
            tiled=True,
        ).astype(jnp.float32)
        final_part = backward_inputs(
            back_part, both[:, :key_width], both[:, key_width:], saved_now, weights[layer]
        )
        grad_a = attention_weight_grads(
            section_id, first_saved[0], final_part[1], second_saved[2], back_part[4]
        )
        reduced[layer] = (grad_a, grad_m, grad_o)
        small[layer] = jnp.concatenate([final_part[2], final_part[3]])
        grads_out[layer] = final_part[0]
        cotangent = brain_float(final_part[0])

    def by_micro(pair):
        moved = swap_cores(jnp.where(first, pair[1], pair[0]))
        return jnp.stack(
            [jnp.where(first, pair[0], moved), jnp.where(first, moved, pair[1])], axis=0
        )[None, :, None]

    layer_outputs = by_micro(outputs)
    input_grads = by_micro(grads_out)
    halves = []
    for zero, one in zip(reduced[0], reduced[1]):
        moved = swap_cores(jnp.where(first, one, zero)).astype(jnp.float32)
        kept = jnp.where(first, zero, one).astype(jnp.float32)
        halves.append((jnp.where(first, kept, moved), jnp.where(first, moved, kept)))
    grad_a = jnp.concatenate(halves[0], axis=0)
    grad_m = jnp.concatenate(halves[1], axis=1)
    grad_o = jnp.concatenate(halves[2], axis=1)
    sums = lax.psum(jnp.stack(small), ("section", "shard", "replica"))
    mine = lax.dynamic_index_in_dim(sums, section_id, 0, keepdims=False)

    def block(values):
        count = values.shape[0] // lax.axis_size("shard")
        return lax.dynamic_slice_in_dim(values, shard_id * count, count, 0)[None]

    query_key = (QUERY_HEADS + KEY_VALUE_HEADS) * HEAD_SIZE
    return (
        layer_outputs,
        input_grads,
        grad_a[None, :, :QKV],
        grad_a[None, :, QKV:],
        grad_m[None],
        grad_o[None],
        block(mine[: 2 * D]),
        block(mine[2 * D : 2 * D + query_key]),
        block(mine[2 * D + query_key :]),
    )


def solution(mesh):
    return jax.shard_map(
        local,
        mesh=mesh,
        in_specs=(
            P("section", None, "replica", "shard", None),
            P(None, "replica", "shard"),
            P("section", "shard", None),
            P("section", "shard", None),
            P("section", "shard", None),
            P("section", "shard", None),
            P("section", "shard"),
            P("section", "shard"),
        ),
        out_specs=(
            P("section", None, "replica", "shard", None),
            P("section", None, "replica", "shard", None),
            P("section", "shard", None),
            P("section", "shard", None),
            P("section", "shard", None),
            P("section", "shard", None),
            P("section", "shard"),
            P("section", "shard"),
            P("section", "shard"),
        ),
        check_vma=False,
    )
```

```python
import math

import jax
import jax.numpy as jnp
from jax import lax
from jax.experimental import pallas as pl
from jax.experimental.pallas import tpu as pltpu
from jax.sharding import PartitionSpec as P

D = 896
QUERY_HEADS = 14
KEY_VALUE_HEADS = 2
HEAD_SIZE = 64
FF = 4864
QKV = 1152


eps_norm = 1e-06
rope_base = 1000000.0


def brain_float(values):
    return values.astype(jnp.bfloat16)


def matmul(first_mat, second_mat):
    return jnp.dot(first_mat, second_mat, preferred_element_type=jnp.float32)


def matmul_left(first_mat, second_mat):
    return lax.dot_general(
        first_mat, second_mat, (((0,), (0,)), ((), ())), preferred_element_type=jnp.float32
    )


def matmul_right(first_mat, second_mat):
    return lax.dot_general(
        first_mat, second_mat, (((1,), (1,)), ((), ())), preferred_element_type=jnp.float32
    )


def rotary_tables(token_pos):
    half_dim = HEAD_SIZE // 2
    frequency = jnp.power(rope_base, -2.0 * jnp.arange(half_dim, dtype=jnp.float32) / HEAD_SIZE)
    angles = token_pos.astype(jnp.float32)[:, None] * frequency[None, :]
    return (jnp.cos(angles)[:, None, :], jnp.sin(angles)[:, None, :])


def rotary_embed(values, cosine_table, sine_values):
    half_dim = values.shape[-1] // 2
    first_half = values[..., :half_dim]
    second_half = values[..., half_dim:]
    return jnp.concatenate(
        [
            first_half * cosine_table - second_half * sine_values,
            second_half * cosine_table + first_half * sine_values,
        ],
        axis=-1,
    )


def rotary_backward(grads, cosine_table, sine_values):
    half_dim = grads.shape[-1] // 2
    first_half = grads[..., :half_dim]
    second_half = grads[..., half_dim:]
    return jnp.concatenate(
        [
            first_half * cosine_table + second_half * sine_values,
            second_half * cosine_table - first_half * sine_values,
        ],
        axis=-1,
    )


def visible(token_pos, row_index, seq_len):
    columns = jnp.arange(seq_len, dtype=jnp.int32)
    return (columns[None, :] <= row_index[:, None]) & (
        columns[None, :] >= (row_index - token_pos)[:, None]
    )


def attention_inputs(block_in, token_pos, weights):
    attn_full, out_full, mlp_full, down_full, gain_full, bias_full = weights
    count_of_rows = block_in.shape[0]
    hidden = block_in.astype(jnp.float32)
    inverse = lax.rsqrt(jnp.mean(hidden * hidden, axis=-1, keepdims=True) + eps_norm)
    normed = brain_float(hidden * inverse * gain_full[:D].astype(jnp.float32))
    project_matrix = matmul(normed, attn_full) + bias_full.astype(jnp.float32)
    cosine_table, sine_values = rotary_tables(token_pos)
    query_rows = brain_float(
        rotary_embed(
            project_matrix[:, : QUERY_HEADS * HEAD_SIZE].reshape(
                count_of_rows, QUERY_HEADS, HEAD_SIZE
            ),
            cosine_table,
            sine_values,
        )
    ).reshape(count_of_rows, QUERY_HEADS * HEAD_SIZE)
    keys_here = brain_float(
        rotary_embed(
            project_matrix[
                :, QUERY_HEADS * HEAD_SIZE : (QUERY_HEADS + KEY_VALUE_HEADS) * HEAD_SIZE
            ].reshape(count_of_rows, KEY_VALUE_HEADS, HEAD_SIZE),
            cosine_table,
            sine_values,
        )
    ).reshape(count_of_rows, KEY_VALUE_HEADS * HEAD_SIZE)
    value_rows_local = brain_float(project_matrix[:, (QUERY_HEADS + KEY_VALUE_HEADS) * HEAD_SIZE :])
    return (normed, inverse, query_rows, keys_here, value_rows_local)


def attention_forward(query_rows, keys_all, value_rows_every, allowed):
    count_of_rows = query_rows.shape[0]
    heads_per_group = QUERY_HEADS // KEY_VALUE_HEADS
    scaling = 1.0 / math.sqrt(HEAD_SIZE)
    grouped_heads = query_rows.reshape(count_of_rows, KEY_VALUE_HEADS, heads_per_group, HEAD_SIZE)
    outputs = []
    logsums = []
    for head_cluster in range(KEY_VALUE_HEADS):
        keys_group = keys_all[:, head_cluster * HEAD_SIZE : (head_cluster + 1) * HEAD_SIZE]
        values_group = value_rows_every[
            :, head_cluster * HEAD_SIZE : (head_cluster + 1) * HEAD_SIZE
        ]
        scores = (
            jnp.einsum(
                "ikd,jd->kij",
                grouped_heads[:, head_cluster],
                keys_group,
                preferred_element_type=jnp.float32,
            )
            * scaling
        )
        masked = jnp.where(allowed[None], scores, -1e30)
        row_max = jnp.max(masked, axis=-1, keepdims=True)
        exponent = jnp.exp(masked - row_max)
        row_sum = jnp.sum(exponent, axis=-1, keepdims=True)
        probability = brain_float(exponent / row_sum)
        outputs.append(
            jnp.einsum("kij,jd->ikd", probability, values_group, preferred_element_type=jnp.float32)
        )
        logsums.append((row_max + jnp.log(row_sum))[..., 0])
    return (
        jnp.stack(outputs, axis=1).reshape(count_of_rows, QUERY_HEADS * HEAD_SIZE),
        jnp.stack(logsums, axis=0),
    )


def attention_backward(query_rows, keys_all, value_rows_every, logsum, attended_gradient, allowed):
    count_of_rows = query_rows.shape[0]
    heads_per_group = QUERY_HEADS // KEY_VALUE_HEADS
    scaling = 1.0 / math.sqrt(HEAD_SIZE)
    grouped_heads = query_rows.reshape(count_of_rows, KEY_VALUE_HEADS, heads_per_group, HEAD_SIZE)
    grouped_gradient = attended_gradient.reshape(
        count_of_rows, KEY_VALUE_HEADS, heads_per_group, HEAD_SIZE
    )
    query_parts = []
    key_parts = []
    value_parts = []
    for head_cluster in range(KEY_VALUE_HEADS):
        keys_group = keys_all[:, head_cluster * HEAD_SIZE : (head_cluster + 1) * HEAD_SIZE]
        values_group = value_rows_every[
            :, head_cluster * HEAD_SIZE : (head_cluster + 1) * HEAD_SIZE
        ]
        scores = (
            jnp.einsum(
                "ikd,jd->kij",
                grouped_heads[:, head_cluster],
                keys_group,
                preferred_element_type=jnp.float32,
            )
            * scaling
        )
        masked = jnp.where(allowed[None], scores, -1e30)
        probability = jnp.exp(masked - logsum[head_cluster][..., None])
        value_parts.append(
            jnp.einsum(
                "kij,ikd->jd",
                brain_float(probability),
                grouped_gradient[:, head_cluster],
                preferred_element_type=jnp.float32,
            )
        )
        prob_grad = jnp.einsum(
            "ikd,jd->kij",
            grouped_gradient[:, head_cluster],
            values_group,
            preferred_element_type=jnp.float32,
        )
        inner_sum = jnp.sum(probability * prob_grad, axis=-1, keepdims=True)
        score_low = brain_float(probability * (prob_grad - inner_sum))
        query_parts.append(
            jnp.einsum("kij,jd->ikd", score_low, keys_group, preferred_element_type=jnp.float32)
            * scaling
        )
        key_parts.append(
            jnp.einsum(
                "kij,ikd->jd",
                score_low,
                grouped_heads[:, head_cluster],
                preferred_element_type=jnp.float32,
            )
            * scaling
        )
    return (
        jnp.stack(query_parts, axis=1).reshape(count_of_rows, QUERY_HEADS * HEAD_SIZE),
        jnp.concatenate(key_parts, axis=1),
        jnp.concatenate(value_parts, axis=1),
    )


def finish_forward(block_in, token_pos, row_index, first_part, keys_all, value_rows_every, weights):
    attn_full, out_full, mlp_full, down_full, gain_full, bias_full = weights
    normed, inverse, query_rows, keys_here, value_rows_local = first_part
    allowed = visible(token_pos, row_index, keys_all.shape[0])
    attended, logsum = attention_forward(query_rows, keys_all, value_rows_every, allowed)
    attended_low = brain_float(attended)
    middle = block_in.astype(jnp.float32) + matmul(attended_low, out_full)
    inverse_two = lax.rsqrt(jnp.mean(middle * middle, axis=-1, keepdims=True) + eps_norm)
    normed_two = brain_float(middle * inverse_two * gain_full[D:].astype(jnp.float32))
    gate_up = matmul(normed_two, mlp_full)
    activated = brain_float(jax.nn.silu(gate_up[:, :FF]) * gate_up[:, FF:])
    result = brain_float(middle + matmul(activated, down_full))
    return (result, logsum, attended_low, middle, inverse_two, normed_two, gate_up, activated)


def backward_mlp(cotangent, saved_now, weights):
    attn_full, out_full, mlp_full, down_full, gain_full, bias_full = weights
    second_part = saved_now[5]
    result, logsum, attended_low, middle, inverse_two, normed_two, gate_up, activated = second_part
    mid_grad = matmul_right(cotangent, down_full)
    gate_in = gate_up[:, :FF]
    upward = gate_up[:, FF:]
    sigmoid_g = jax.nn.sigmoid(gate_in)
    gate_grad = mid_grad * upward * sigmoid_g * (1.0 + gate_in * (1.0 - sigmoid_g))
    up_grad = mid_grad * gate_in * sigmoid_g
    gate_up_low = brain_float(jnp.concatenate([gate_grad, up_grad], axis=1))
    normed_grad = matmul_right(gate_up_low, mlp_full)
    return (gate_up_low, normed_grad)


def backward_branches(cotangent, mlp_part, saved_now, row_index, weights):
    attn_full, out_full, mlp_full, down_full, gain_full, bias_full = weights
    block_in, token_pos, first_part, keys_all, value_rows_every, second_part = saved_now
    normed, inverse, query_rows, keys_here, value_rows_local = first_part
    result, logsum, attended_low, middle, inverse_two, normed_two, gate_up, activated = second_part
    gate_up_low, normed_grad = mlp_part
    plain_two = middle * inverse_two
    gain_grad_two = jnp.sum(normed_grad * plain_two, axis=0)
    scaled_two = normed_grad * gain_full[D:].astype(jnp.float32)
    middle_grad = cotangent.astype(jnp.float32) + inverse_two * (
        scaled_two - plain_two * jnp.mean(scaled_two * plain_two, axis=-1, keepdims=True)
    )
    branch_low = brain_float(middle_grad)
    attended_gradient = brain_float(matmul_right(branch_low, out_full))
    allowed = visible(token_pos, row_index, keys_all.shape[0])
    query_grad, key_part, value_part = attention_backward(
        query_rows, keys_all, value_rows_every, logsum, attended_gradient, allowed
    )
    return (query_grad, key_part, value_part, middle_grad, branch_low, gate_up_low, gain_grad_two)


def backward_inputs(back_part, key_gradients, value_grads, saved_now, weights):
    attn_full, out_full, mlp_full, down_full, gain_full, bias_full = weights
    block_in, token_pos, first_part, keys_all, value_rows_every, second_part = saved_now
    normed, inverse, query_rows, keys_here, value_rows_local = first_part
    query_grad, key_part, value_part, middle_grad, branch_low, gate_up_low, gain_grad_two = (
        back_part
    )
    count_of_rows = block_in.shape[0]
    cosine_table, sine_values = rotary_tables(token_pos)
    query_back = rotary_backward(
        query_grad.reshape(count_of_rows, QUERY_HEADS, HEAD_SIZE), cosine_table, sine_values
    ).reshape(count_of_rows, QUERY_HEADS * HEAD_SIZE)
    key_backward = rotary_backward(
        key_gradients.reshape(count_of_rows, KEY_VALUE_HEADS, HEAD_SIZE), cosine_table, sine_values
    ).reshape(count_of_rows, KEY_VALUE_HEADS * HEAD_SIZE)
    project_low = brain_float(jnp.concatenate([query_back, key_backward, value_grads], axis=1))
    bias_grad = jnp.sum(project_low, axis=0, dtype=jnp.float32)
    normed_grad = matmul_right(project_low, attn_full)
    plain_one = block_in.astype(jnp.float32) * inverse
    gain_grad_one = jnp.sum(normed_grad * plain_one, axis=0)
    scaled_one = normed_grad * gain_full[:D].astype(jnp.float32)
    input_grad = middle_grad + inverse * (
        scaled_one - plain_one * jnp.mean(scaled_one * plain_one, axis=-1, keepdims=True)
    )
    return (input_grad, project_low, jnp.concatenate([gain_grad_one, gain_grad_two]), bias_grad)


MESH = pl.DeviceIdType.MESH


def gather_kernel(
    a_in, m_in, o_in, a_out, m_out, o_out, here, zs, zr, rs, rr, ds, dr, own_s, own_r, cs, cr
):
    section = lax.axis_index("section")
    shard = lax.axis_index("shard")
    replica = lax.axis_index("replica")
    nz = lax.axis_size("shard")
    other = 1 - section
    near = replica + 1 - 2 * lax.rem(replica, 2)
    far = lax.rem(replica + 2, 4)
    across = 3 - replica
    a_cols = a_in.shape[1] // 4
    m_cols = m_in.shape[2] // 4

    def piece(p, layer, z, q):
        if p == 0:
            return a_out.at[layer, z, :, pl.ds(pl.multiple_of(q * a_cols, 128), a_cols)]
        if p == 3:
            return o_out.at[layer, z, q]
        return m_out.at[layer, z, p - 1, :, pl.ds(pl.multiple_of(q * m_cols, 128), m_cols)]

    def source(p, q):
        if p == 0:
            return a_in.at[:, pl.ds(pl.multiple_of(q * a_cols, 128), a_cols)]
        if p == 3:
            return o_in.at[q]
        return m_in.at[p - 1, :, pl.ds(pl.multiple_of(q * m_cols, 128), m_cols)]

    def remote(src, dst, send, recv, target):
        return pltpu.make_async_remote_copy(
            src_ref=src,
            dst_ref=dst,
            send_sem=send,
            recv_sem=recv,
            device_id=target,
            device_id_type=MESH,
        )

    barrier = pltpu.get_barrier_semaphore()
    peers = [{"shard": lax.rem(shard + k, nz)} for k in range(1, nz)]
    peers += [{"replica": near}, {"replica": far}, {"section": other}]
    for peer in peers:
        pl.semaphore_signal(barrier, inc=1, device_id=peer, device_id_type=MESH)
    pl.semaphore_wait(barrier, len(peers))

    order = sorted(range(1, nz), key=lambda k: min(k, nz - k))
    sent = []

    def along(p, k):
        return remote(
            source(p, replica),
            piece(p, section, shard, replica),
            zs.at[p, k],
            zr.at[p, k],
            {"shard": lax.rem(shard + k, nz)},
        )

    for p in range(4):
        for k in order:
            copy = along(p, k)
            copy.start()
            sent.append(copy)
    wholes = (
        (a_in, a_out.at[section, shard], a_out.at[other, shard]),
        (m_in, m_out.at[section, shard], m_out.at[other, shard]),
        (o_in, o_out.at[section, shard], o_out.at[other, shard]),
    )
    locals_here = []
    arrivals = []
    for index, (src, dst, landing) in enumerate(wholes):
        copy = pltpu.make_async_copy(src, dst, here.at[index])
        copy.start()
        locals_here.append(copy)
        copy = remote(src, dst, own_s.at[index], own_r.at[index], {"section": other})
        copy.start()
        sent.append(copy)
        arrivals.append(
            remote(src, landing, own_s.at[index], own_r.at[index], {"section": other})
        )

    def to_core(p, k, kind, q):
        z = lax.rem(shard + nz - k, nz)
        ref = piece(p, section, z, q)
        copy = remote(ref, ref, cs.at[kind, p, k], cr.at[kind, p, k], {"section": other})
        copy.start()
        sent.append(copy)
        landing = piece(p, other, z, q)
        arrivals.append(
            remote(
                landing, landing, cs.at[kind, p, k], cr.at[kind, p, k], {"section": other}
            )
        )

    def first_hop(p, k):
        z = lax.rem(shard + nz - k, nz)
        ref = piece(p, section, z, replica)
        remote(ref, ref, zs.at[p, k], zr.at[p, k], {"shard": z}).wait_recv()
        for way, target in enumerate((near, far)):
            copy = remote(ref, ref, rs.at[way, p, k], rr.at[way, p, k], {"replica": target})
            copy.start()
            sent.append(copy)
        to_core(p, k, 0, replica)

    def second_hop(p, k):
        z = lax.rem(shard + nz - k, nz)
        by_near = (p + (k if p in (0, 3) else 0)) % 2 == 0
        for way, (origin, target) in enumerate(((near, far), (far, near))):
            ref = piece(p, section, z, origin)
            remote(
                ref, ref, rs.at[way, p, k], rr.at[way, p, k], {"replica": origin}
            ).wait_recv()
            if by_near == (way == 0):
                copy = remote(ref, ref, ds.at[p, k], dr.at[p, k], {"replica": target})
                copy.start()
                sent.append(copy)
            to_core(p, k, 1 + way, origin)

    def third_hop(p, k):
        z = lax.rem(shard + nz - k, nz)
        ref = piece(p, section, z, across)
        by_near = (p + (k if p in (0, 3) else 0)) % 2 == 0
        origin = far if by_near else near
        remote(ref, ref, ds.at[p, k], dr.at[p, k], {"replica": origin}).wait_recv()
        to_core(p, k, 3, across)

    for step in range(6):
        if step < 4:
            for k in order:
                first_hop(step, k)
        if 1 <= step < 5:
            for k in order:
                second_hop(step - 1, k)
        if step >= 2:
            for k in order:
                third_hop(step - 2, k)
    for copy in arrivals:
        copy.wait_recv()
    for copy in sent:
        copy.wait_send()
    for copy in locals_here:
        copy.wait()


def gather_weights(attn_in, out_proj, mlp_in, mlp_out):
    nz = lax.axis_size("shard")
    joined = jnp.concatenate([attn_in, out_proj], axis=1)
    rows, a_cols = joined.shape
    m_cols = mlp_in.shape[1]
    down_rows, d_model = mlp_out.shape
    m_in = mlp_in.reshape(2, rows // 2, m_cols)
    o_in = mlp_out.reshape(4, down_rows // 4, d_model)
    dma = pltpu.SemaphoreType.DMA
    a_all, m_all, o_all = pl.pallas_call(
        gather_kernel,
        out_shape=(
            jax.ShapeDtypeStruct((2, nz) + joined.shape, jnp.bfloat16),
            jax.ShapeDtypeStruct((2, nz) + m_in.shape, jnp.bfloat16),
            jax.ShapeDtypeStruct((2, nz) + o_in.shape, jnp.bfloat16),
        ),
        in_specs=[pl.BlockSpec(memory_space=pl.ANY)] * 3,
        out_specs=(pl.BlockSpec(memory_space=pl.ANY),) * 3,
        scratch_shapes=[
            dma((3,)),
            dma((4, nz)),
            dma((4, nz)),
            dma((2, 4, nz)),
            dma((2, 4, nz)),
            dma((4, nz)),
            dma((4, nz)),
            dma((3,)),
            dma((3,)),
            dma((4, 4, nz)),
            dma((4, 4, nz)),
        ],
        compiler_params=pltpu.CompilerParams(collective_id=0, has_side_effects=True),
    )(joined, m_in, o_in)
    return (
        a_all.reshape(2, nz * rows, a_cols),
        m_all.reshape(2, nz * rows, m_cols),
        o_all.reshape(2, nz * down_rows, d_model),
    )


def swap_cores(value):
    return lax.ppermute(value, "section", [(0, 1), (1, 0)])


def scatter_shards(value):
    nz = lax.axis_size("shard")
    shard = lax.axis_index("shard")
    total = lax.dynamic_index_in_dim(value, shard, 0, keepdims=False).astype(jnp.float32)
    for k in range(1, nz):
        block = lax.dynamic_index_in_dim(value, lax.rem(shard + k, nz), 0, keepdims=False)
        block = lax.ppermute(block, "shard", [(i, (i + k) % nz) for i in range(nz)])
        total = total + block.astype(jnp.float32)
    return brain_float(total)


def reduce_group(send, keep):
    half = brain_float(keep.astype(jnp.float32) + swap_cores(send).astype(jnp.float32))
    part = lax.psum_scatter(half, "replica", scatter_dimension=0, tiled=True)
    nz = lax.axis_size("shard")
    block = scatter_shards(part.reshape(nz, part.shape[0] // nz, part.shape[1]))
    replica = lax.axis_index("replica")
    rows = block.shape[0]
    whole = jnp.zeros((4 * rows, block.shape[1]), block.dtype)
    for mask in range(4):
        part = block
        if mask > 0:
            part = lax.ppermute(block, "replica", [(i, i ^ mask) for i in range(4)])
        place = jnp.bitwise_xor(replica, mask) * rows
        whole = lax.dynamic_update_slice_in_dim(whole, part, place, 0)
    return whole


def replica_major(values, inner):
    nz = lax.axis_size("shard")
    rows = values.shape[0]
    width = values.shape[1] // (inner * 4 * nz)
    return (
        values.reshape(rows, nz, inner, 4, width)
        .transpose(0, 2, 3, 1, 4)
        .reshape(rows, values.shape[1])
    )


def picked(section_id, first, second):
    return jnp.where(section_id == 0, second, first), jnp.where(section_id == 0, first, second)


def mlp_weight_grads(section_id, normed_two, gate_up_low, activated, cotangent):
    nz = lax.axis_size("shard")
    normed_two = replica_major(normed_two, 1)
    send, keep = picked(section_id, gate_up_low[:, :FF], gate_up_low[:, FF:])
    grad_m = reduce_group(
        brain_float(matmul_left(normed_two, send)), brain_float(matmul_left(normed_two, keep))
    )
    send, keep = picked(section_id, cotangent[:, : D // 2], cotangent[:, D // 2 :])

    def down(half):
        grad = brain_float(matmul_left(activated, half))
        rows = grad.shape[0]
        return (
            grad.reshape(nz, 4, rows // (4 * nz), D // 2).transpose(1, 0, 2, 3).reshape(rows, D // 2)
        )

    return grad_m, reduce_group(down(send), down(keep))


def attention_weight_grads(section_id, normed, project_low, attended_low, branch_low):
    normed = replica_major(normed, 2)
    attended_low = replica_major(attended_low, 2)
    normed_send, normed_keep = picked(section_id, normed[:, : D // 2], normed[:, D // 2 :])
    attended_send, attended_keep = picked(
        section_id, attended_low[:, : D // 2], attended_low[:, D // 2 :]
    )

    def grads(first, second):
        return brain_float(
            jnp.concatenate(
                [matmul_left(first, project_low), matmul_left(second, branch_low)], axis=1
            )
        )

    return reduce_group(grads(normed_send, attended_send), grads(normed_keep, attended_keep))


def local(edges, positions, attn_in, out_proj, mlp_in, mlp_out, gains, bias):
    section_id = lax.axis_index("section")
    shard_id = lax.axis_index("shard")
    count_of_rows = edges.shape[3]
    first = section_id == 0
    own = edges[0, :, 0]
    incoming = swap_cores(jnp.where(first, own[1], own[0]))
    block_in = jnp.where(first, own[0], incoming)
    cotangent = jnp.where(first, incoming, own[1])
    token_pos = lax.dynamic_index_in_dim(positions[:, 0], section_id, 0, keepdims=False)
    row_index = shard_id * count_of_rows + jnp.arange(count_of_rows, dtype=jnp.int32)
    gain_rows = gains.shape[1]
    vectors = lax.all_gather(
        jnp.concatenate([gains[0], bias[0]]), ("section", "shard"), axis=0, tiled=False
    ).reshape(2, -1, gain_rows + bias.shape[1])
    gain_full = vectors[:, :, :gain_rows].reshape(2, -1)
    bias_full = vectors[:, :, gain_rows:].reshape(2, -1)
    a_all, m_all, o_all = gather_weights(attn_in[0], out_proj[0], mlp_in[0], mlp_out[0])
    weights = [
        (a_all[l][:, :QKV], a_all[l][:, QKV:], m_all[l], o_all[l], gain_full[l], bias_full[l])
        for l in range(2)
    ]
    saved_all = []
    outputs = []
    key_width = KEY_VALUE_HEADS * HEAD_SIZE
    for layer in range(2):
        first_part = attention_inputs(block_in, token_pos, weights[layer])
        both = lax.all_gather(
            jnp.concatenate([first_part[3], first_part[4]], axis=1), "shard", axis=0, tiled=True
        )
        keys_all, values_all = both[:, :key_width], both[:, key_width:]
        second_part = finish_forward(
            block_in, token_pos, row_index, first_part, keys_all, values_all, weights[layer]
        )
        saved_all.append((block_in, token_pos, first_part, keys_all, values_all, second_part))
        block_in = second_part[0]
        outputs.append(block_in)
    grads_out = [None, None]
    reduced = [None, None]
    small = [None, None]
    for layer in (1, 0):
        saved_now = saved_all[layer]
        first_saved, second_saved = saved_now[2], saved_now[5]
        mlp_part = backward_mlp(cotangent, saved_now, weights[layer])
        grad_m, grad_o = mlp_weight_grads(
            section_id, second_saved[5], mlp_part[0], second_saved[7], cotangent
        )
        back_part = backward_branches(cotangent, mlp_part, saved_now, row_index, weights[layer])
        both = lax.psum_scatter(
            brain_float(jnp.concatenate([back_part[1], back_part[2]], axis=1)),
            "shard",
            scatter_dimension=0,
            tiled=True,
        ).astype(jnp.float32)
        final_part = backward_inputs(
            back_part, both[:, :key_width], both[:, key_width:], saved_now, weights[layer]
        )
        grad_a = attention_weight_grads(
            section_id, first_saved[0], final_part[1], second_saved[2], back_part[4]
        )
        reduced[layer] = (grad_a, grad_m, grad_o)
        small[layer] = jnp.concatenate([final_part[2], final_part[3]])
        grads_out[layer] = final_part[0]
        cotangent = brain_float(final_part[0])

    def by_micro(pair):
        moved = swap_cores(jnp.where(first, pair[1], pair[0]))
        return jnp.stack(
            [jnp.where(first, pair[0], moved), jnp.where(first, moved, pair[1])], axis=0
        )[None, :, None]

    layer_outputs = by_micro(outputs)
    input_grads = by_micro(grads_out)
    halves = []
    for zero, one in zip(reduced[0], reduced[1]):
        moved = swap_cores(jnp.where(first, one, zero)).astype(jnp.float32)
        kept = jnp.where(first, zero, one).astype(jnp.float32)
        halves.append((jnp.where(first, kept, moved), jnp.where(first, moved, kept)))
    grad_a = jnp.concatenate(halves[0], axis=0)
    grad_m = jnp.concatenate(halves[1], axis=1)
    grad_o = jnp.concatenate(halves[2], axis=1)
    sums = lax.psum(jnp.stack(small), ("section", "shard", "replica"))
    mine = lax.dynamic_index_in_dim(sums, section_id, 0, keepdims=False)

    def block(values):
        count = values.shape[0] // lax.axis_size("shard")
        return lax.dynamic_slice_in_dim(values, shard_id * count, count, 0)[None]

    query_key = (QUERY_HEADS + KEY_VALUE_HEADS) * HEAD_SIZE
    return (
        layer_outputs,
        input_grads,
        grad_a[None, :, :QKV],
        grad_a[None, :, QKV:],
        grad_m[None],
        grad_o[None],
        block(mine[: 2 * D]),
        block(mine[2 * D : 2 * D + query_key]),
        block(mine[2 * D + query_key :]),
    )


def solution(mesh):
    return jax.shard_map(
        local,
        mesh=mesh,
        in_specs=(
            P("section", None, "replica", "shard", None),
            P(None, "replica", "shard"),
            P("section", "shard", None),
            P("section", "shard", None),
            P("section", "shard", None),
            P("section", "shard", None),
            P("section", "shard"),
            P("section", "shard"),
        ),
        out_specs=(
            P("section", None, "replica", "shard", None),
            P("section", None, "replica", "shard", None),
            P("section", "shard", None),
            P("section", "shard", None),
            P("section", "shard", None),
            P("section", "shard", None),
            P("section", "shard"),
            P("section", "shard"),
            P("section", "shard"),
        ),
        check_vma=False,
    )
```
